1024 devices in a mesh: dp: 16 (over x, y), expert: 64 (over z, core).
Axes of the slice: x: 4, y: 4, z: 32, core: 2. Of those that a mesh axis runs over, the one named last changes fastest.
Arguments:
- grad_out: bfloat16 [2048, 4096], P('expert', 'dp'), may hold values from -6 to 6
- routes: int32 [2048, 8], P('expert'), may hold values from 0 to 63, all different within a row; in each aligned block of 32 rows (0 to 31, 32 to 63, ...) at most 8 rows name the same one
- route_weight: float32 [2048, 8], P('expert'), may hold values from 0.2 to 1
- saved_input: bfloat16 [64, 512, 4096], P('expert', None, 'dp'), may hold values from -6 to 6
- saved_gate: bfloat16 [64, 512, 1024], P('expert'), may hold values from -6 to 6
- saved_up: bfloat16 [64, 512, 1024], P('expert'), may hold values from -6 to 6
- w_gate: bfloat16 [64, 4096, 1024], P('expert', 'dp'), may hold values from -0.09375 to 0.09375
- w_up: bfloat16 [64, 4096, 1024], P('expert', 'dp'), may hold values from -0.09375 to 0.09375
- w_down: bfloat16 [64, 1024, 4096], P('expert', None, 'dp'), may hold values from -0.1875 to 0.1875
Outputs:
- grad_in: bfloat16 [2048, 4096], P('expert', 'dp')
- grad_gate: bfloat16 [64, 4096, 1024], P('expert', 'dp')
- grad_up: bfloat16 [64, 4096, 1024], P('expert', 'dp')
- grad_down: bfloat16 [64, 1024, 4096], P('expert', None, 'dp')
The draws below stay inside these ranges and needn't reach their ends.
Inputs may be any that keep to these rules, and one draw needn't show every extreme that they name: `routes`: each token names 8 different experts. Among the tokens of one block of 32 no expert is named by more than 8 tokens, and in every draw some expert is named by exactly 8 tokens of some block.
All inputs are finite; a program needn't handle non-finite values.
Results may differ from the reference program's by a relative error of at most 0.023.
Values may be sent and summed in bfloat16 or wider, within the bound.
A program may use at most 32 MiB of HBM per device.

```python
import math
import jax
import jax.numpy as jnp
import numpy as np
from jax import lax

D = 4096
H = 1024
TOP = 8
TOK_DEV = 32
EXPERTS = 64
CAP = 8
SLOTS = 512
TOKENS = 2048
N_DP = 16


def level_of(own_key, extent, cuts, low, high):
    gain = 1.0
    for position, blocks in cuts:
        draws = jax.random.uniform(jax.random.fold_in(jax.random.fold_in(own_key, 6), position), (blocks,), jnp.float32, low / len(cuts), high / len(cuts))
        gain = gain * jnp.repeat(jnp.exp(draws), extent[position] // blocks).reshape((-1,) + (1,) * (len(extent) - 1 - position))
    return gain


def routed_block(stream_key, own, number, rows, number_of, top, bound, slope):
    order = jax.random.permutation(stream_key, number_of)
    heavy_load, usual = shares(number_of, rows * top, bound, slope, True), shares(number_of, rows * top, bound, slope, False)
    places = jnp.arange(number_of)

    def named(tallies, offset_by):
        used = int((tallies > 0).sum())
        fixed = max(1, used // 4)
        shifted = fixed + (places - fixed + offset_by * (used - fixed)) % max(1, number_of - fixed)
        return jnp.zeros((number_of,), jnp.int32).at[order[jnp.where(places < fixed, places, shifted)]].set(jnp.asarray(tallies, jnp.int32))

    tallies = jnp.where(number % 4 == 0, named(heavy_load, number // 4), named(usual, number - number // 4 - 1))
    mixed = jax.random.permutation(jax.random.fold_in(own, 3), number_of)
    giver, taker = mixed[0:number_of // 2 * 2:2], mixed[1:number_of // 2 * 2:2]
    room = jnp.minimum(tallies[giver] - 1, bound - tallies[taker]) // 2
    room = jnp.where((giver == order[0]) | (taker == order[0]) | (tallies[taker] == 0), 0, jnp.maximum(room, 0))
    shifted = jax.random.randint(jax.random.fold_in(own, 4), (number_of // 2,), 0, 1 << 20) % (room + 1)
    tallies = tallies.at[giver].add(-shifted).at[taker].add(shifted)
    labels = jnp.searchsorted(jnp.cumsum(tallies), jnp.arange(rows * top), side="right").astype(jnp.int32)
    table = labels.reshape(top, rows).T
    table = table[jax.random.permutation(jax.random.fold_in(own, 1), rows)]
    offset_by = jax.random.randint(jax.random.fold_in(own, 2), (rows, 1), 0, top)
    return jnp.take_along_axis(table, (jnp.arange(top)[None, :] + offset_by) % top, axis=1)


def shares(amount, total, most, skew, full):
    weights = [(1 << 20) // math.isqrt(rank ** skew) + 1 for rank in range(1, amount + 1)]
    largest = most if full else min(most, max(-(-total // amount), total * weights[0] // sum(weights)))
    least = 1 if total - largest >= amount - 1 else 0
    given, rest = [largest] + [least] * (amount - 1), total - largest - least * (amount - 1)
    while rest > 0:
        free = [i for i in range(1, amount) if given[i] < largest] or [i for i in range(1, amount) if given[i] < most]
        mass, left = sum([weights[i] for i in free]), rest
        for i in free:
            more = min(most - given[i], max(1, left * weights[i] // mass), rest)
            given[i] = given[i] + more
            rest = rest - more
    return np.array(given)


def normal_values(key, extent, width, limit, shards=(), held_as=jnp.bfloat16):
    values = width * jax.random.normal(key, extent, jnp.float32)
    if shards:
        values = values * level_of(key, extent, shards, -0.22, 0.18)
    return jnp.clip(values, -limit, limit).astype(held_as)


def setup_inputs(seed: int = 0) -> dict:
    key_of = jax.random.split(jax.random.key(seed), 10)
    grad_out = normal_values(key_of[0], (TOKENS, D), 1.0, 6.0, ((0, 64), (1, 16)))
    routes_keys = jax.random.split(jax.random.fold_in(key_of[1], 1), TOKENS // TOK_DEV)
    routes_turns = jax.random.permutation(jax.random.fold_in(key_of[1], 3), TOKENS // TOK_DEV)
    routes = jax.vmap(lambda own, number: routed_block(jax.random.fold_in(key_of[1], 2), own, number, TOK_DEV, EXPERTS, TOP, CAP, 2))(routes_keys, routes_turns).reshape((TOKENS, TOP))
    route_weight = jnp.clip(0.2 + 0.8 * jax.random.uniform(key_of[2], (TOKENS, TOP), jnp.float32) ** level_of(key_of[2], (TOKENS, TOP), ((0, 64),), -0.2, 0.2), 0.2, 1.0)
    saved_input = normal_values(key_of[3], (EXPERTS, SLOTS, D), 1.0, 6.0, ((0, 64), (2, 16)))
    saved_gate = normal_values(key_of[4], (EXPERTS, SLOTS, H), 1.0, 6.0, ((0, 64),))
    saved_up = normal_values(key_of[5], (EXPERTS, SLOTS, H), 1.0, 6.0, ((0, 64),))
    w_gate = normal_values(key_of[6], (EXPERTS, D, H), D ** -0.5, 0.09375, ((0, 64), (1, 16)))
    w_up = normal_values(key_of[7], (EXPERTS, D, H), D ** -0.5, 0.09375, ((0, 64), (1, 16)))
    w_down = normal_values(key_of[8], (EXPERTS, H, D), H ** -0.5, 0.1875, ((0, 64), (2, 16)))
    return dict(grad_out=grad_out, routes=routes, route_weight=route_weight, saved_input=saved_input, saved_gate=saved_gate, saved_up=saved_up, w_gate=w_gate, w_up=w_up, w_down=w_down)


def slot_targets(routes):
    blocks = routes.reshape(TOKENS // TOK_DEV, TOK_DEV * TOP)
    onehot = (blocks[:, :, None] == jnp.arange(EXPERTS, dtype=jnp.int32)[None, None, :]).astype(jnp.int32)
    before = jnp.cumsum(onehot, axis=1) - onehot
    ranks = jnp.sum(before * onehot, axis=2)
    source = jnp.arange(TOKENS // TOK_DEV, dtype=jnp.int32)[:, None]
    return (blocks * SLOTS + source * CAP + ranks).reshape(-1).astype(jnp.int32)


def expert_backward(operands):
    slot_grads, inputs, gate_saved, up_saved, gate_weight, up_weight, down_weight = operands
    grouped_grads = slot_grads.astype(jnp.float32).reshape(SLOTS, N_DP, D // N_DP)
    grouped_down = down_weight.astype(jnp.float32).reshape(H, N_DP, D // N_DP)
    partials = jnp.einsum("sgd,hgd->gsh", grouped_grads, grouped_down).astype(jnp.bfloat16)
    partials = lax.optimization_barrier(partials)
    hidden_grad = jnp.sum(partials.astype(jnp.float32), axis=0)
    gate_full = gate_saved.astype(jnp.float32)
    up_full = up_saved.astype(jnp.float32)
    sigmoid_g = jax.nn.sigmoid(gate_full)
    silu_g = gate_full * sigmoid_g
    hidden = (silu_g * up_full).astype(jnp.bfloat16)
    d_gate = (hidden_grad * up_full * sigmoid_g * (1.0 + gate_full * (1.0 - sigmoid_g))).astype(jnp.bfloat16)
    d_up = (hidden_grad * silu_g).astype(jnp.bfloat16)
    slot_input = (jnp.dot(d_gate, gate_weight.T, preferred_element_type=jnp.float32)
                  + jnp.dot(d_up, up_weight.T, preferred_element_type=jnp.float32)).astype(jnp.bfloat16)
    grad_gate = jnp.dot(inputs.T, d_gate, preferred_element_type=jnp.float32).astype(jnp.bfloat16)
    grad_up = jnp.dot(inputs.T, d_up, preferred_element_type=jnp.float32).astype(jnp.bfloat16)
    grad_down = jnp.dot(hidden.T, slot_grads, preferred_element_type=jnp.float32).astype(jnp.bfloat16)
    return slot_input, grad_gate, grad_up, grad_down


def reference(grad_out, routes, route_weight, saved_input, saved_gate, saved_up, w_gate, w_up, w_down):
    targets = slot_targets(routes)
    scaled = (route_weight[:, :, None] * grad_out[:, None, :].astype(jnp.float32)).astype(jnp.bfloat16)
    slots = jnp.zeros((EXPERTS * SLOTS, D), jnp.bfloat16).at[targets].set(scaled.reshape(-1, D))
    slots = slots.reshape(EXPERTS, SLOTS, D)
    slot_input, grad_gate, grad_up, grad_down = lax.map(
        expert_backward, (slots, saved_input, saved_gate, saved_up, w_gate, w_up, w_down))
    picked = slot_input.reshape(EXPERTS * SLOTS, D)[targets].astype(jnp.float32)
    grad_in = jnp.sum(picked.reshape(TOKENS, TOP, D), axis=1).astype(jnp.bfloat16)
    return grad_in, grad_gate, grad_up, grad_down
```

```python
import jax
import jax.numpy as jnp
from jax import lax
from jax.experimental import pallas as pl
from jax.experimental.pallas import tpu as pltpu
from jax.sharding import PartitionSpec as P

MESH = pl.DeviceIdType.MESH
F32 = jnp.float32
BF16 = jnp.bfloat16

CHUNKS = (
    (0, 1, -1, 2, -2, 3, -3, 6),
    (-6, 4, 5, 7, 8, 9, -4, -5),
    (-7, -8, -9, 12, -12, 10, 11, 13),
    (14, 15, 16, -10, -11, -13, -14, -15),
)
ORDER = tuple(o for chunk in CHUNKS for o in chunk)
PLACE = {o: i for i, o in enumerate(ORDER)}
TREE = {
    0: (6, -6, 3, -3, 2, -2, 1, -1),
    6: (12, 9, 8, 7, 5, 4),
    -6: (-12, -9, -8, -7, -5, -4),
    12: (16, 15, 14, 13, 11, 10),
    -12: (-15, -14, -13, -11, -10),
}
PARENT = {o: k for k, kids in TREE.items() for o in kids}
NEAR = (1, -1, 2, -2, 3, -3, 4, -4, 6, -6)
NCH = len(CHUNKS)
LAST = (((1,), (1,)), ((), ()))
FIRST = (((0,), (0,)), ((), ()))


def kernel(
    n_dp,
    n_z,
    tok_ref,
    meta_ref,
    xin_ref,
    gate_ref,
    up_ref,
    wg_ref,
    wu_ref,
    wd_ref,
    gin_out,
    gg_out,
    gu_out,
    gd_out,
    buf,
    xin,
    gate,
    up,
    wg,
    wu,
    wd,
    fac_a,
    fac_b,
    hid,
    sel,
    sg,
    part,
    rsr,
    hg,
    dg,
    du,
    contr,
    sb,
    ssum,
    rb,
    gin,
    gg,
    gu,
    gd,
    lsem,
    osem,
    zs,
    zr,
    bs,
    br,
    rss,
    rsrs,
    ags,
    agr,
    cs,
    cr,
    zs2,
    zr2,
):
    d = lax.axis_index("dp")
    e = lax.axis_index("expert")
    z = e // 2
    c = e % 2
    x = d // 4
    y = d % 4

    def chip(o):
        return (d, ((z + (o + n_z)) % n_z) * 2 + c)

    sibling = (d, z * 2 + (1 - c))

    def peer(j):
        return (((x + j // 4) % 4) * 4 + (y + j % 4) % 4, e)

    def remote(src, dst, s, r, dev):
        return pltpu.make_async_remote_copy(
            src_ref=src, dst_ref=dst, send_sem=s, recv_sem=r, device_id=dev, device_id_type=MESH
        )

    barrier = pltpu.get_barrier_semaphore()
    for o in (6, -6, 4, -4, 3, -3, 2, -2, 1, -1):
        pl.semaphore_signal(barrier, inc=1, device_id=chip(o), device_id_type=MESH)
    for j in range(1, n_dp):
        pl.semaphore_signal(barrier, inc=1, device_id=peer(j), device_id_type=MESH)
    pl.semaphore_signal(barrier, inc=1, device_id=sibling, device_id_type=MESH)

    own = [
        pltpu.make_async_copy(tok_ref.at[:, pl.ds(0, 128)], buf.at[0, c, pl.ds(0, 32)], lsem.at[0]),
        pltpu.make_async_copy(tok_ref.at[:, pl.ds(128, 128)], buf.at[0, c, pl.ds(32, 32)], lsem.at[1]),
        pltpu.make_async_copy(meta_ref, buf.at[0, c, pl.ds(64, 16)], lsem.at[2]),
    ]
    for cp in own:
        cp.start()
    for i, o in enumerate(ORDER):
        rows = pl.ds(pl.multiple_of(((z + (o + n_z)) % n_z) * 16, 16), 16)
        pltpu.make_async_copy(gate_ref.at[rows], gate.at[pl.ds(16 * i, 16)], lsem.at[3]).start()
        pltpu.make_async_copy(up_ref.at[rows], up.at[pl.ds(16 * i, 16)], lsem.at[4]).start()
        pltpu.make_async_copy(xin_ref.at[rows], xin.at[pl.ds(16 * i, 16)], lsem.at[5]).start()
    load_wd = pltpu.make_async_copy(wd_ref, wd, lsem.at[6])
    load_wg = pltpu.make_async_copy(wg_ref, wg, lsem.at[7])
    load_wu = pltpu.make_async_copy(wu_ref, wu, lsem.at[8])
    load_wd.start()
    load_wg.start()
    load_wu.start()
    for cp in own:
        cp.wait()
    pl.semaphore_wait(barrier, len(NEAR) + n_dp)

    def hop(o):
        k = PARENT[o]
        i = PLACE[o]
        return remote(buf.at[PLACE[k], c], buf.at[i, c], zs.at[i], zr.at[i], chip(k - o))

    def relay(k):
        for o in TREE[k]:
            hop(o).start()

    def share(g):
        block = buf.at[pl.ds(8 * g, 8), c]
        return remote(block, block, bs.at[g], br.at[g], sibling)

    def arrived(g, skip=()):
        for o in CHUNKS[g]:
            if o not in skip:
                hop(o).wait_recv()

    relay(0)

    pltpu.make_async_copy(gate_ref, gate, lsem.at[3]).wait()
    pltpu.make_async_copy(up_ref, up, lsem.at[4]).wait()

    @pl.loop(0, 32)
    def _(i):
        rows = pl.ds(pl.multiple_of(i * 16, 16), 16)
        g32 = gate[rows, :].astype(F32)
        u32 = up[rows, :].astype(F32)
        s = 1.0 / (1.0 + jnp.exp(-g32))
        silu = g32 * s
        fac_b[rows, :] = silu
        fac_a[rows, :] = u32 * s * (1.0 + g32 * (1.0 - s))
        hid[rows, :] = (silu * u32).astype(BF16)

    line = lax.broadcasted_iota(jnp.int32, (128, 768), 0)
    lane = lax.broadcasted_iota(jnp.int32, (128, 768), 1)
    tok_of = lane & 31
    kind = lane >> 8
    spread = (
        ((kind == 0) & (line < tok_of))
        | ((kind == 1) & (line == tok_of))
        | ((kind == 2) & (line >= 32) & ((line & 31) == tok_of))
    )
    spread = jnp.where(spread, 1.0, 0.0).astype(BF16)
    e32 = e.astype(F32)
    load_wd.wait()

    def scatter(g):
        tags = buf[pl.ds(8 * g, 8), :, pl.ds(64, 16), :].reshape(16, 16, 128).astype(F32)
        hit = tags[:, 0:8, :] == e32
        found = jnp.sum(jnp.where(hit, tags[:, 8:16, :], 0.0), axis=1)
        wide = jnp.dot(found.astype(BF16), spread, preferred_element_type=F32)
        row8 = lax.broadcasted_iota(jnp.int32, (8, 768), 0)
        lane8 = lax.broadcasted_iota(jnp.int32, (8, 768), 1)
        mine = ((lane8 & 255) >> 5) == row8
        for q in range(2):
            flat = jnp.sum(jnp.where(mine, wide[8 * q : 8 * q + 8, :], 0.0), axis=0, keepdims=True)
            rank = flat[:, 0:256]
            there = flat[:, 256:512]
            weight = flat[:, 512:768]
            group = (lax.broadcasted_iota(jnp.int32, (1, 256), 1) >> 5) * 8
            key = jnp.where(there > 0.5, group.astype(F32) + rank, -1.0)
            slot = lax.broadcasted_iota(jnp.int32, (64, 256), 0).astype(F32)
            pick = slot == key
            scale = jnp.sum(jnp.where(pick, weight, 0.0), axis=1, keepdims=True)
            one = jnp.where(pick, 1.0, 0.0).astype(BF16)
            sel[2 * g + q] = one
            base = 8 * g + 4 * q
            low = buf[pl.ds(base, 4), :, pl.ds(0, 32), :].reshape(256, 128)
            high = buf[pl.ds(base, 4), :, pl.ds(32, 32), :].reshape(256, 128)
            rows = pl.ds(16 * base, 64)
            sg[rows, 0:128] = (jnp.dot(one, low, preferred_element_type=F32) * scale).astype(BF16)
            sg[rows, 128:256] = (jnp.dot(one, high, preferred_element_type=F32) * scale).astype(BF16)
        grads = sg[pl.ds(128 * g, 128), :]
        for h in range(2):
            sums = lax.dot_general(grads, wd[pl.ds(512 * h, 512), :], LAST, preferred_element_type=F32)
            part[g, :, h] = sums.astype(BF16).reshape(8, 16, 512)

    def rs(g, j):
        dev = peer(j)
        p = dev[0]
        return remote(part.at[g, p // 2, p % 2], rsr.at[g, j], rss.at[g, j], rsrs.at[g, j], dev)

    def ag(g, j):
        piece = hg.at[g, d // 2, d % 2]
        return remote(piece, piece, ags.at[g, j], agr.at[g, j], peer(j))

    def rs_start(g):
        @pl.loop(1, n_dp)
        def _(j):
            rs(g, j).start()

    def reduce(g):
        @pl.loop(1, n_dp)
        def _(j):
            rs(g, j).wait_recv()

        total = part[g, d // 2, d % 2].astype(F32)
        for j in range(1, n_dp):
            total = total + rsr[g, j].astype(F32)
        hg[g, d // 2, d % 2] = total.astype(BF16)

        @pl.loop(1, n_dp)
        def _(j):
            ag(g, j).start()

    def local(g):
        @pl.loop(1, n_dp)
        def _(j):
            ag(g, j).wait_recv()

        rows = pl.ds(128 * g, 128)
        for h in range(2):
            cols = pl.ds(512 * h, 512)
            grad = hg[g, :, h].reshape(128, 512).astype(F32)
            dg[rows, cols] = (grad * fac_a[rows, cols]).astype(BF16)
            du[rows, cols] = (grad * fac_b[rows, cols]).astype(BF16)
        out = lax.dot_general(dg[rows, :], wg[...], LAST, preferred_element_type=F32)
        out = out + lax.dot_general(du[rows, :], wu[...], LAST, preferred_element_type=F32)
        out = out.astype(BF16)
        for q in range(2):
            dense = lax.dot_general(
                sel[2 * g + q], out[64 * q : 64 * q + 64, :], FIRST, preferred_element_type=F32
            )
            contr[pl.ds(8 * g + 4 * q, 4)] = dense.astype(BF16).reshape(4, 2, 32, 256)
        pair(g).start()

    def pair(g):
        block = pl.ds(8 * g, 8)
        return remote(contr.at[block, 1 - c], sb.at[block], cs.at[g], cr.at[g], sibling)

    def back(o):
        k = PARENT[o]
        i = PLACE[o]
        return remote(ssum.at[i], rb.at[i], zs2.at[i], zr2.at[i], chip(o - k))

    def join(g):
        pair(g).wait_recv()
        block = pl.ds(8 * g, 8)
        ssum[block] = (contr[block, c].astype(F32) + sb[block].astype(F32)).astype(BF16)
        for o in CHUNKS[g]:
            if o not in TREE:
                back(o).start()

    def gather(k):
        total = ssum[PLACE[k]].astype(F32)
        for o in TREE[k][::-1]:
            back(o).wait_recv()
            total = total + rb[PLACE[o]].astype(F32)
        return total

    hop(6).wait_recv()
    relay(6)
    hop(-6).wait_recv()
    relay(-6)
    for o in CHUNKS[0]:
        if o not in TREE:
            hop(o).wait_recv()
    share(0).start()
    share(0).wait_recv()
    scatter(0)
    rs_start(0)
    for o in CHUNKS[1]:
        if o not in TREE:
            hop(o).wait_recv()
    share(1).start()
    hop(12).wait_recv()
    relay(12)
    hop(-12).wait_recv()
    relay(-12)
    share(1).wait_recv()
    scatter(1)
    rs_start(1)
    reduce(0)
    for g in (2, 3):
        for o in CHUNKS[g]:
            if o not in TREE:
                hop(o).wait_recv()
        share(g).start()
    for g in (2, 3):
        share(g).wait_recv()
        scatter(g)
        rs_start(g)
    reduce(1)
    load_wg.wait()
    load_wu.wait()
    local(0)
    reduce(2)
    reduce(3)
    local(1)
    join(0)
    local(2)
    join(1)
    local(3)
    join(2)
    join(3)
    for k in (12, -12):
        ssum[PLACE[k]] = gather(k).astype(BF16)
        back(k).start()

    pltpu.make_async_copy(xin_ref, xin, lsem.at[5]).wait()

    @pl.loop(0, 4)
    def _(i):
        cols = pl.ds(pl.multiple_of(i * 256, 256), 256)
        gg[:, cols] = lax.dot_general(
            xin[...], dg[:, cols], FIRST, preferred_element_type=F32
        ).astype(BF16)
        gu[:, cols] = lax.dot_general(
            xin[...], du[:, cols], FIRST, preferred_element_type=F32
        ).astype(BF16)
        gd[cols, :] = lax.dot_general(
            hid[:, cols], sg[...], FIRST, preferred_element_type=F32
        ).astype(BF16)

    outs = [
        pltpu.make_async_copy(gg, gg_out, osem.at[0]),
        pltpu.make_async_copy(gu, gu_out, osem.at[1]),
        pltpu.make_async_copy(gd, gd_out, osem.at[2]),
    ]
    for cp in outs:
        cp.start()
    for k in (6, -6):
        ssum[PLACE[k]] = gather(k).astype(BF16)
        back(k).start()
    gin[...] = gather(0).astype(BF16)
    last = pltpu.make_async_copy(gin, gin_out, osem.at[3])
    last.start()

    for o in ORDER:
        if o != 0:
            hop(o).wait_send()
            back(o).wait_send()
    for g in range(NCH):
        share(g).wait_send()
        pair(g).wait_send()

        @pl.loop(1, n_dp)
        def _(j):
            rs(g, j).wait_send()
            ag(g, j).wait_send()

    for cp in outs:
        cp.wait()
    last.wait()


def solution(mesh):
    n_dp = mesh.shape["dp"]
    n_z = mesh.shape["expert"] // 2

    def on_device(grad_out, routes, route_weight, saved_input, saved_gate, saved_up, w_gate, w_up, w_down):
        named = jnp.tile(routes.T.astype(F32), (1, 4))
        w = route_weight.T
        top = lax.reduce_precision(w, 8, 7)
        rest = w - top
        mid = lax.reduce_precision(rest, 8, 7)
        low = rest - mid
        values = jnp.concatenate([jnp.ones_like(w), top, mid, low], axis=1)
        meta = jnp.concatenate([named, values], axis=0).astype(BF16)
        anywhere = pl.BlockSpec(memory_space=pl.ANY)
        dma = pltpu.SemaphoreType.DMA
        vm = pltpu.VMEM
        grads = pl.pallas_call(
            lambda *refs: kernel(n_dp, n_z, *refs),
            out_shape=(
                jax.ShapeDtypeStruct((32, 256), BF16),
                jax.ShapeDtypeStruct((256, 1024), BF16),
                jax.ShapeDtypeStruct((256, 1024), BF16),
                jax.ShapeDtypeStruct((1024, 256), BF16),
            ),
            in_specs=[anywhere] * 8,
            out_specs=[anywhere] * 4,
            scratch_shapes=[
                vm((32, 2, 80, 128), BF16),
                vm((512, 256), BF16),
                vm((512, 1024), BF16),
                vm((512, 1024), BF16),
                vm((256, 1024), BF16),
                vm((256, 1024), BF16),
                vm((1024, 256), BF16),
                vm((512, 1024), F32),
                vm((512, 1024), F32),
                vm((512, 1024), BF16),
                vm((8, 64, 256), BF16),
                vm((512, 256), BF16),
                vm((NCH, 8, 2, 16, 512), BF16),
                vm((NCH, 16, 16, 512), BF16),
                vm((NCH, 8, 2, 16, 512), BF16),
                vm((512, 1024), BF16),
                vm((512, 1024), BF16),
                vm((32, 2, 32, 256), BF16),
                vm((32, 32, 256), BF16),
                vm((32, 32, 256), BF16),
                vm((32, 32, 256), BF16),
                vm((32, 256), BF16),
                vm((256, 1024), BF16),
                vm((256, 1024), BF16),
                vm((1024, 256), BF16),
                dma((9,)),
                dma((4,)),
                dma((32,)),
                dma((32,)),
                dma((NCH,)),
                dma((NCH,)),
                dma((NCH, 16)),
                dma((NCH, 16)),
                dma((NCH, 16)),
                dma((NCH, 16)),
                dma((NCH,)),
                dma((NCH,)),
                dma((32,)),
                dma((32,)),
            ],
            name="expert_backward",
            compiler_params=pltpu.CompilerParams(
                collective_id=0, has_side_effects=True, vmem_limit_bytes=44 * 1024 * 1024
            ),
        )(
            grad_out,
            meta,
            saved_input[0],
            saved_gate[0],
            saved_up[0],
            w_gate[0],
            w_up[0],
            w_down[0],
        )
        grad_in, grad_gate, grad_up, grad_down = grads
        return (grad_in, grad_gate[None], grad_up[None], grad_down[None])

    in_specs = (
        P("expert", "dp"),
        P("expert", None),
        P("expert", None),
        P("expert", None, "dp"),
        P("expert", None, None),
        P("expert", None, None),
        P("expert", "dp", None),
        P("expert", "dp", None),
        P("expert", None, "dp"),
    )
    out_specs = (
        P("expert", "dp"),
        P("expert", "dp", None),
        P("expert", "dp", None),
        P("expert", None, "dp"),
    )
    return jax.shard_map(
        on_device, mesh=mesh, in_specs=in_specs, out_specs=out_specs, check_vma=False
    )
```

```python
import jax
import jax.numpy as jnp
from jax import lax
from jax.experimental import pallas as pl
from jax.experimental.pallas import tpu as pltpu
from jax.sharding import PartitionSpec as P

MESH = pl.DeviceIdType.MESH
F32 = jnp.float32
BF16 = jnp.bfloat16

CHUNKS = (
    (0, 1, -1, 2, -2, 3, -3, 6),
    (-6, 5, -5, 7, -7, 8, -8, 4),
    (-4, 9, -9, 12, -12, 11, -11, 13),
    (-13, 14, -14, 10, -10, 15, -15, 16),
)
ORDER = tuple(o for chunk in CHUNKS for o in chunk)
PLACE = {o: i for i, o in enumerate(ORDER)}
TREE = {
    0: (6, -6, 2, -2, 1, -1),
    2: (3,),
    -2: (-3,),
    6: (12, 8, 5, 7),
    -6: (-12, -8, -5, -7),
    5: (4,),
    -5: (-4,),
    8: (9,),
    -8: (-9,),
    12: (14, 11, 13),
    -12: (-14, -11, -13),
    14: (16, 15),
    -14: (-15,),
    11: (10,),
    -11: (-10,),
}
PARENT = {o: k for k, kids in TREE.items() for o in kids}
NEAR = (6, -6, 2, -2, 1, -1)
NCH = len(CHUNKS)
LAST = (((1,), (1,)), ((), ()))
FIRST = (((0,), (0,)), ((), ()))


def kernel(
    n_dp,
    n_z,
    tok_ref,
    named_ref,
    weight_ref,
    xin_ref,
    gate_ref,
    up_ref,
    wg_ref,
    wu_ref,
    wd_ref,
    gin_out,
    gg_out,
    gu_out,
    gd_out,
    buf,
    xin_by_chip,
    xin,
    gate,
    up,
    wg,
    wu,
    wd,
    fac_a,
    fac_b,
    hid,
    sel,
    sg,
    part,
    rsr,
    hg,
    dg,
    du,
    contr,
    sb,
    ssum,
    rb,
    gin,
    gg,
    gu,
    gd,
    lsem,
    osem,
    zs,
    zr,
    bs,
    br,
    rss,
    rsrs,
    ags,
    agr,
    cs,
    cr,
    zs2,
    zr2,
):
    d = lax.axis_index("dp")
    e = lax.axis_index("expert")
    z = e // 2
    c = e % 2
    x = d // 4
    y = d % 4

    def chip(o):
        return (d, ((z + (o + n_z)) % n_z) * 2 + c)

    def rows_of(o):
        return pl.ds(pl.multiple_of(((z + (o + n_z)) % n_z) * 16, 16), 16)

    sibling = (d, z * 2 + (1 - c))

    def peer(j):
        return (((x + j // 4) % 4) * 4 + (y + j % 4) % 4, e)

    def remote(src, dst, s, r, dev):
        return pltpu.make_async_remote_copy(
            src_ref=src, dst_ref=dst, send_sem=s, recv_sem=r, device_id=dev, device_id_type=MESH
        )

    barrier = pltpu.get_barrier_semaphore()
    for o in NEAR:
        pl.semaphore_signal(barrier, inc=1, device_id=chip(o), device_id_type=MESH)
    for j in range(1, n_dp):
        pl.semaphore_signal(barrier, inc=1, device_id=peer(j), device_id_type=MESH)
    pl.semaphore_signal(barrier, inc=1, device_id=sibling, device_id_type=MESH)

    own = [
        pltpu.make_async_copy(tok_ref.at[:, pl.ds(0, 128)], buf.at[0, c, pl.ds(0, 32)], lsem.at[0]),
        pltpu.make_async_copy(tok_ref.at[:, pl.ds(128, 128)], buf.at[0, c, pl.ds(32, 32)], lsem.at[1]),
    ]
    for cp in own:
        cp.start()
    load_gate = pltpu.make_async_copy(gate_ref, gate, lsem.at[3])
    load_up = pltpu.make_async_copy(up_ref, up, lsem.at[4])
    load_xin = pltpu.make_async_copy(xin_ref, xin_by_chip, lsem.at[5])
    load_wd = pltpu.make_async_copy(wd_ref, wd, lsem.at[6])
    load_wg = pltpu.make_async_copy(wg_ref, wg, lsem.at[7])
    load_wu = pltpu.make_async_copy(wu_ref, wu, lsem.at[8])
    for cp in (load_gate, load_up, load_wd, load_wg, load_wu, load_xin):
        cp.start()

    token = lax.broadcasted_iota(jnp.int32, (32, 128), 0)
    lane = lax.broadcasted_iota(jnp.int32, (32, 128), 1)
    match = (lane & 31) == token

    def lay(values, where):
        copy = jnp.where(where, 1.0, 0.0).astype(BF16)
        return jnp.dot(values, copy, preferred_element_type=F32)

    weight = weight_ref[...]
    top = weight.astype(BF16)
    rest = weight - top.astype(F32)
    mid = rest.astype(BF16)
    low = (rest - mid.astype(F32)).astype(BF16)
    kind = lane >> 5
    names = lay(named_ref[...].astype(F32).astype(BF16), match)
    terms = lay(top, match & (kind == 1)) + lay(mid, match & (kind == 2)) + lay(low, match & (kind == 3))
    terms = jnp.where(lax.broadcasted_iota(jnp.int32, (8, 128), 1) < 32, 1.0, terms)
    buf[0, c, 64:80, :] = jnp.concatenate([names, terms], axis=0).astype(BF16)
    for cp in own:
        cp.wait()
    pl.semaphore_wait(barrier, len(NEAR) + n_dp)

    def hop(o):
        k = PARENT[o]
        i = PLACE[o]
        return remote(buf.at[PLACE[k], c], buf.at[i, c], zs.at[0], zr.at[i], chip(k - o))

    def relay(k):
        for o in TREE[k]:
            hop(o).start()

    def share(g):
        block = buf.at[pl.ds(8 * g, 8), c]
        return remote(block, block, bs.at[g], br.at[g], sibling)

    relay(0)

    load_gate.wait()
    load_up.wait()
    for i, o in enumerate(ORDER):
        there = rows_of(o)
        rows = pl.ds(16 * i, 16)
        g32 = gate[there, :].astype(F32)
        u32 = up[there, :].astype(F32)
        s = 1.0 / (1.0 + jnp.exp(-g32))
        silu = g32 * s
        fac_b[rows, :] = silu
        fac_a[rows, :] = u32 * s * (1.0 + g32 * (1.0 - s))
        hid[rows, :] = (silu * u32).astype(BF16)

    line = lax.broadcasted_iota(jnp.int32, (128, 768), 0)
    lane = lax.broadcasted_iota(jnp.int32, (128, 768), 1)
    tok_of = lane & 31
    kind = lane >> 8
    spread = (
        ((kind == 0) & (line < tok_of))
        | ((kind == 1) & (line == tok_of))
        | ((kind == 2) & (line >= 32) & ((line & 31) == tok_of))
    )
    spread = jnp.where(spread, 1.0, 0.0).astype(BF16)
    e32 = e.astype(F32)
    load_wd.wait()

    def scatter(g):
        tags = buf[pl.ds(8 * g, 8), :, pl.ds(64, 16), :].reshape(16, 16, 128).astype(F32)
        hit = tags[:, 0:8, :] == e32
        found = jnp.sum(jnp.where(hit, tags[:, 8:16, :], 0.0), axis=1)
        wide = jnp.dot(found.astype(BF16), spread, preferred_element_type=F32)
        row8 = lax.broadcasted_iota(jnp.int32, (8, 768), 0)
        lane8 = lax.broadcasted_iota(jnp.int32, (8, 768), 1)
        mine = ((lane8 & 255) >> 5) == row8
        for q in range(2):
            flat = jnp.sum(jnp.where(mine, wide[8 * q : 8 * q + 8, :], 0.0), axis=0, keepdims=True)
            rank = flat[:, 0:256]
            there = flat[:, 256:512]
            weight = flat[:, 512:768]
            group = (lax.broadcasted_iota(jnp.int32, (1, 256), 1) >> 5) * 8
            key = jnp.where(there > 0.5, group.astype(F32) + rank, -1.0)
            slot = lax.broadcasted_iota(jnp.int32, (64, 256), 0).astype(F32)
            pick = slot == key
            scale = jnp.sum(jnp.where(pick, weight, 0.0), axis=1, keepdims=True)
            one = jnp.where(pick, 1.0, 0.0).astype(BF16)
            sel[2 * g + q] = one
            base = 8 * g + 4 * q
            low = buf[pl.ds(base, 4), :, pl.ds(0, 32), :].reshape(256, 128)
            high = buf[pl.ds(base, 4), :, pl.ds(32, 32), :].reshape(256, 128)
            rows = pl.ds(16 * base, 64)
            sg[rows, 0:128] = (jnp.dot(one, low, preferred_element_type=F32) * scale).astype(BF16)
            sg[rows, 128:256] = (jnp.dot(one, high, preferred_element_type=F32) * scale).astype(BF16)
        grads = sg[pl.ds(128 * g, 128), :]
        for h in range(2):
            sums = lax.dot_general(grads, wd[pl.ds(512 * h, 512), :], LAST, preferred_element_type=F32)
            part[g, :, h] = sums.astype(BF16).reshape(8, 16, 512)

    def rs(g, j):
        dev = peer(j)
        p = dev[0]
        return remote(part.at[g, p // 2, p % 2], rsr.at[g, j], rss.at[g], rsrs.at[g], dev)

    def ag(g, j):
        piece = hg.at[g, d // 2, d % 2]
        return remote(piece, piece, ags.at[g], agr.at[g], peer(j))

    def rs_start(g):
        @pl.loop(1, n_dp)
        def _(j):
            rs(g, j).start()

    def rs_all(g):
        block = rsr.at[g, pl.ds(1, n_dp - 1)]
        return remote(block, block, rss.at[g], rsrs.at[g], sibling)

    def ag_all(g):
        block = rsr.at[g, pl.ds(1, n_dp - 1)]
        return remote(block, block, ags.at[g], agr.at[g], sibling)

    def reduce(g):
        rs_all(g).wait_recv()
        total = part[g, d // 2, d % 2].astype(F32)
        for j in range(1, n_dp):
            total = total + rsr[g, j].astype(F32)
        hg[g, d // 2, d % 2] = total.astype(BF16)

        @pl.loop(1, n_dp)
        def _(j):
            ag(g, j).start()

    def local(g):
        ag_all(g).wait_recv()
        rows = pl.ds(128 * g, 128)
        for h in range(2):
            cols = pl.ds(512 * h, 512)
            grad = hg[g, :, h].reshape(128, 512).astype(F32)
            dg[rows, cols] = (grad * fac_a[rows, cols]).astype(BF16)
            du[rows, cols] = (grad * fac_b[rows, cols]).astype(BF16)
        out = lax.dot_general(dg[rows, :], wg[...], LAST, preferred_element_type=F32)
        out = out + lax.dot_general(du[rows, :], wu[...], LAST, preferred_element_type=F32)
        out = out.astype(BF16)
        for q in range(2):
            dense = lax.dot_general(
                sel[2 * g + q], out[64 * q : 64 * q + 64, :], FIRST, preferred_element_type=F32
            )
            contr[pl.ds(8 * g + 4 * q, 4)] = dense.astype(BF16).reshape(4, 2, 32, 256)
        pair(g).start()

    def pair(g):
        block = pl.ds(8 * g, 8)
        return remote(contr.at[block, 1 - c], sb.at[block], cs.at[g], cr.at[g], sibling)

    def back(o):
        k = PARENT[o]
        i = PLACE[o]
        return remote(ssum.at[i], rb.at[i], zs2.at[0], zr2.at[i], chip(o - k))

    def join(g):
        pair(g).wait_recv()
        block = pl.ds(8 * g, 8)
        ssum[block] = (contr[block, c].astype(F32) + sb[block].astype(F32)).astype(BF16)
        for o in CHUNKS[g]:
            if o not in TREE:
                back(o).start()

    def forward(*ks):
        for k in ks:
            ssum[PLACE[k]] = gather(k).astype(BF16)
            back(k).start()

    def gather(k):
        total = ssum[PLACE[k]].astype(F32)
        for o in TREE[k][::-1]:
            back(o).wait_recv()
            total = total + rb[PLACE[o]].astype(F32)
        return total

    def pass_on(*ks):
        for k in ks:
            hop(k).wait_recv()
            relay(k)

    def leaves(g):
        for o in CHUNKS[g]:
            if o not in TREE:
                hop(o).wait_recv()
        share(g).start()

    pass_on(2, -2, 6, -6)
    leaves(0)
    share(0).wait_recv()
    scatter(0)
    rs_start(0)
    pass_on(8, -8, 5, -5)
    leaves(1)
    pass_on(12, -12)
    share(1).wait_recv()
    scatter(1)
    rs_start(1)
    pass_on(14, -14, 11, -11)
    leaves(2)
    reduce(0)
    share(2).wait_recv()
    scatter(2)
    rs_start(2)
    leaves(3)
    reduce(1)
    share(3).wait_recv()
    scatter(3)
    rs_start(3)
    load_wg.wait()
    load_wu.wait()
    local(0)
    reduce(2)
    join(0)
    local(1)
    reduce(3)
    join(1)
    local(2)
    join(2)
    local(3)
    forward(5, -5, 8, -8, 2, -2)
    join(3)
    forward(14, -14, 11, -11, 12, -12)

    load_xin.wait()
    for i, o in enumerate(ORDER):
        xin[pl.ds(16 * i, 16), :] = xin_by_chip[rows_of(o), :]

    @pl.loop(0, 4)
    def _(i):
        cols = pl.ds(pl.multiple_of(i * 256, 256), 256)
        gg[:, cols] = lax.dot_general(
            xin[...], dg[:, cols], FIRST, preferred_element_type=F32
        ).astype(BF16)
        gu[:, cols] = lax.dot_general(
            xin[...], du[:, cols], FIRST, preferred_element_type=F32
        ).astype(BF16)
        gd[cols, :] = lax.dot_general(
            hid[:, cols], sg[...], FIRST, preferred_element_type=F32
        ).astype(BF16)

    outs = [
        pltpu.make_async_copy(gg, gg_out, osem.at[0]),
        pltpu.make_async_copy(gu, gu_out, osem.at[1]),
        pltpu.make_async_copy(gd, gd_out, osem.at[2]),
    ]
    for cp in outs:
        cp.start()
    hops = buf.at[pl.ds(1, n_z - 1), c]
    remote(hops, hops, zs.at[0], zr.at[0], sibling).wait_send()
    for g in range(NCH):
        share(g).wait_send()
        pair(g).wait_send()
        rs_all(g).wait_send()
        ag_all(g).wait_send()
    forward(6, -6)
    gin[...] = gather(0).astype(BF16)
    last = pltpu.make_async_copy(gin, gin_out, osem.at[3])
    last.start()

    hops = rb.at[pl.ds(1, n_z - 1)]
    remote(hops, hops, zs2.at[0], zr2.at[0], sibling).wait_send()
    for cp in outs:
        cp.wait()
    last.wait()


def hand_over(*refs):
    sources, targets, held, sem = refs[:4], refs[4:8], refs[8:12], refs[12]
    loads, stores = [], []
    for i in range(4):
        parts = 2 if i else 1
        rows = sources[i].shape[0] // parts
        for part in range(parts):
            block = pl.ds(rows * part, rows)
            here = held[i].at[block]
            loads.append(pltpu.make_async_copy(sources[i].at[block], here, sem.at[0, i, part]))
            stores.append(pltpu.make_async_copy(here, targets[i].at[block], sem.at[1, i, part]))
    for load in loads:
        load.start()
    for load, store in zip(loads, stores):
        load.wait()
        store.start()
    for store in stores:
        store.wait()


def solution(mesh):
    n_dp = mesh.shape["dp"]
    n_z = mesh.shape["expert"] // 2

    def on_device(grad_out, routes, route_weight, saved_input, saved_gate, saved_up, w_gate, w_up, w_down):
        anywhere = pl.BlockSpec(memory_space=pl.ANY)
        dma = pltpu.SemaphoreType.DMA
        vm = pltpu.VMEM
        grads = pl.pallas_call(
            lambda *refs: kernel(n_dp, n_z, *refs),
            out_shape=(
                jax.ShapeDtypeStruct((32, 256), BF16),
                jax.ShapeDtypeStruct((256, 1024), BF16),
                jax.ShapeDtypeStruct((256, 1024), BF16),
                jax.ShapeDtypeStruct((1024, 256), BF16),
            ),
            in_specs=[anywhere] + [pl.BlockSpec(memory_space=pltpu.VMEM)] * 2 + [anywhere] * 6,
            out_specs=[anywhere] * 4,
            scratch_shapes=[
                vm((32, 2, 80, 128), BF16),
                vm((512, 256), BF16),
                vm((512, 256), BF16),
                vm((512, 1024), BF16),
                vm((512, 1024), BF16),
                vm((256, 1024), BF16),
                vm((256, 1024), BF16),
                vm((1024, 256), BF16),
                vm((512, 1024), F32),
                vm((512, 1024), F32),
                vm((512, 1024), BF16),
                vm((8, 64, 256), BF16),
                vm((512, 256), BF16),
                vm((NCH, 8, 2, 16, 512), BF16),
                vm((NCH, 16, 16, 512), BF16),
                vm((NCH, 8, 2, 16, 512), BF16),
                vm((512, 1024), BF16),
                vm((512, 1024), BF16),
                vm((32, 2, 32, 256), BF16),
                vm((32, 32, 256), BF16),
                vm((32, 32, 256), BF16),
                vm((32, 32, 256), BF16),
                vm((32, 256), BF16),
                vm((256, 1024), BF16),
                vm((256, 1024), BF16),
                vm((1024, 256), BF16),
                dma((9,)),
                dma((4,)),
                dma((1,)),
                dma((32,)),
                dma((NCH,)),
                dma((NCH,)),
                dma((NCH,)),
                dma((NCH,)),
                dma((NCH,)),
                dma((NCH,)),
                dma((NCH,)),
                dma((NCH,)),
                dma((1,)),
                dma((32,)),
            ],
            name="expert_backward",
            compiler_params=pltpu.CompilerParams(
                collective_id=0, has_side_effects=True, vmem_limit_bytes=56 * 1024 * 1024
            ),
        )(
            grad_out,
            routes.T,
            route_weight.T,
            saved_input[0],
            saved_gate[0],
            saved_up[0],
            w_gate[0],
            w_up[0],
            w_down[0],
        )
        grad_in, grad_gate, grad_up, grad_down = pl.pallas_call(
            hand_over,
            out_shape=tuple(jax.ShapeDtypeStruct(a.shape, a.dtype) for a in grads),
            in_specs=[anywhere] * 4,
            out_specs=[anywhere] * 4,
            scratch_shapes=[vm(a.shape, a.dtype) for a in grads] + [dma((2, 4, 2))],
            name="hand_over",
            compiler_params=pltpu.CompilerParams(vmem_limit_bytes=56 * 1024 * 1024),
        )(*grads)
        return (grad_in, grad_gate[None], grad_up[None], grad_down[None])

    in_specs = (
        P("expert", "dp"),
        P("expert", None),
        P("expert", None),
        P("expert", None, "dp"),
        P("expert", None, None),
        P("expert", None, None),
        P("expert", "dp", None),
        P("expert", "dp", None),
        P("expert", None, "dp"),
    )
    out_specs = (
        P("expert", "dp"),
        P("expert", "dp", None),
        P("expert", "dp", None),
        P("expert", None, "dp"),
    )
    return jax.shard_map(
        on_device, mesh=mesh, in_specs=in_specs, out_specs=out_specs, check_vma=False
    )
```

```python
import jax
import jax.numpy as jnp
from jax import lax
from jax.experimental import pallas as pl
from jax.experimental.pallas import tpu as pltpu
from jax.sharding import PartitionSpec as P

MESH = pl.DeviceIdType.MESH
F32 = jnp.float32
BF16 = jnp.bfloat16

CHUNKS = (
    (0, 1, -1, 2, -2, 3, -3, 6),
    (-6, 5, -5, 7, -7, 8, -8, 4),
    (-4, 9, -9, 12, -12, 11, -11, 13),
    (-13, 14, -14, 10, -10, 15, -15, 16),
)
ORDER = tuple(o for chunk in CHUNKS for o in chunk)
PLACE = {o: i for i, o in enumerate(ORDER)}
TREE = {
    0: (6, -6, 2, -2, 1, -1),
    2: (3,),
    -2: (-3,),
    6: (12, 8, 5, 7),
    -6: (-12, -8, -5, -7),
    5: (4,),
    -5: (-4,),
    8: (9,),
    -8: (-9,),
    12: (14, 11, 13),
    -12: (-14, -11, -13),
    14: (16, 15),
    -14: (-15,),
    11: (10,),
    -11: (-10,),
}
PARENT = {o: k for k, kids in TREE.items() for o in kids}
NEAR = (6, -6, 2, -2, 1, -1)
NCH = len(CHUNKS)
LAST = (((1,), (1,)), ((), ()))
FIRST = (((0,), (0,)), ((), ()))


def kernel(
    n_dp,
    n_z,
    tok_ref,
    named_ref,
    weight_ref,
    xin_ref,
    gate_ref,
    up_ref,
    wg_ref,
    wu_ref,
    wd_ref,
    gin_out,
    gg_out,
    gu_out,
    gd_out,
    buf,
    xin_by_chip,
    xin,
    gate,
    up,
    wg,
    wu,
    wd,
    fac_a,
    fac_b,
    hid,
    sel,
    sg,
    part,
    rsr,
    hg,
    dg,
    du,
    contr,
    sb,
    ssum,
    rb,
    gin,
    gg,
    gu,
    gd,
    lsem,
    osem,
    zs,
    zr,
    bs,
    br,
    rss,
    rsrs,
    ags,
    agr,
    cs,
    cr,
    zs2,
    zr2,
):
    d = lax.axis_index("dp")
    e = lax.axis_index("expert")
    z = e // 2
    c = e % 2
    x = d // 4
    y = d % 4

    def chip(o):
        return (d, ((z + (o + n_z)) % n_z) * 2 + c)

    def rows_of(o):
        return pl.ds(pl.multiple_of(((z + (o + n_z)) % n_z) * 16, 16), 16)

    sibling = (d, z * 2 + (1 - c))

    def peer(j):
        return (((x + j // 4) % 4) * 4 + (y + j % 4) % 4, e)

    def remote(src, dst, s, r, dev):
        return pltpu.make_async_remote_copy(
            src_ref=src, dst_ref=dst, send_sem=s, recv_sem=r, device_id=dev, device_id_type=MESH
        )

    barrier = pltpu.get_barrier_semaphore()
    for o in NEAR:
        pl.semaphore_signal(barrier, inc=1, device_id=chip(o), device_id_type=MESH)
    for j in range(1, n_dp):
        pl.semaphore_signal(barrier, inc=1, device_id=peer(j), device_id_type=MESH)
    pl.semaphore_signal(barrier, inc=1, device_id=sibling, device_id_type=MESH)

    own = [
        pltpu.make_async_copy(tok_ref.at[:, pl.ds(0, 128)], buf.at[0, c, pl.ds(0, 32)], lsem.at[0]),
        pltpu.make_async_copy(tok_ref.at[:, pl.ds(128, 128)], buf.at[0, c, pl.ds(32, 32)], lsem.at[1]),
    ]
    for cp in own:
        cp.start()
    load_gate = pltpu.make_async_copy(gate_ref, gate, lsem.at[3])
    load_up = pltpu.make_async_copy(up_ref, up, lsem.at[4])
    load_xin = pltpu.make_async_copy(xin_ref, xin_by_chip, lsem.at[5])
    load_wd = pltpu.make_async_copy(wd_ref, wd, lsem.at[6])
    load_wg = pltpu.make_async_copy(wg_ref, wg, lsem.at[7])
    load_wu = pltpu.make_async_copy(wu_ref, wu, lsem.at[8])
    for cp in (load_gate, load_up, load_wd, load_wg, load_wu, load_xin):
        cp.start()

    token = lax.broadcasted_iota(jnp.int32, (32, 128), 0)
    lane = lax.broadcasted_iota(jnp.int32, (32, 128), 1)
    match = (lane & 31) == token

    def lay(values, where):
        copy = jnp.where(where, 1.0, 0.0).astype(BF16)
        return jnp.dot(values, copy, preferred_element_type=F32)

    weight = weight_ref[...]
    top = weight.astype(BF16)
    rest = weight - top.astype(F32)
    mid = rest.astype(BF16)
    low = (rest - mid.astype(F32)).astype(BF16)
    kind = lane >> 5
    names = lay(named_ref[...].astype(F32).astype(BF16), match)
    terms = lay(top, match & (kind == 1)) + lay(mid, match & (kind == 2)) + lay(low, match & (kind == 3))
    terms = jnp.where(lax.broadcasted_iota(jnp.int32, (8, 128), 1) < 32, 1.0, terms)
    buf[0, c, 64:80, :] = jnp.concatenate([names, terms], axis=0).astype(BF16)
    for cp in own:
        cp.wait()
    pl.semaphore_wait(barrier, len(NEAR) + n_dp)

    def hop(o):
        k = PARENT[o]
        i = PLACE[o]
        return remote(buf.at[PLACE[k], c], buf.at[i, c], zs.at[0], zr.at[i], chip(k - o))

    def relay(k):
        for o in TREE[k]:
            hop(o).start()

    def share(g):
        block = buf.at[pl.ds(8 * g, 8), c]
        return remote(block, block, bs.at[g], br.at[g], sibling)

    relay(0)

    load_gate.wait()
    load_up.wait()
    for i, o in enumerate(ORDER):
        there = rows_of(o)
        rows = pl.ds(16 * i, 16)
        g32 = gate[there, :].astype(F32)
        u32 = up[there, :].astype(F32)
        s = 1.0 / (1.0 + jnp.exp(-g32))
        silu = g32 * s
        fac_b[rows, :] = silu
        fac_a[rows, :] = u32 * s * (1.0 + g32 * (1.0 - s))
        hid[rows, :] = (silu * u32).astype(BF16)

    line = lax.broadcasted_iota(jnp.int32, (128, 768), 0)
    lane = lax.broadcasted_iota(jnp.int32, (128, 768), 1)
    tok_of = lane & 31
    kind = lane >> 8
    spread = (
        ((kind == 0) & (line < tok_of))
        | ((kind == 1) & (line == tok_of))
        | ((kind == 2) & (line >= 32) & ((line & 31) == tok_of))
    )
    spread = jnp.where(spread, 1.0, 0.0).astype(BF16)
    e32 = e.astype(F32)
    load_wd.wait()

    def scatter(g):
        tags = buf[pl.ds(8 * g, 8), :, pl.ds(64, 16), :].reshape(16, 16, 128).astype(F32)
        hit = tags[:, 0:8, :] == e32
        found = jnp.sum(jnp.where(hit, tags[:, 8:16, :], 0.0), axis=1)
        wide = jnp.dot(found.astype(BF16), spread, preferred_element_type=F32)
        row8 = lax.broadcasted_iota(jnp.int32, (8, 768), 0)
        lane8 = lax.broadcasted_iota(jnp.int32, (8, 768), 1)
        mine = ((lane8 & 255) >> 5) == row8
        for q in range(2):
            flat = jnp.sum(jnp.where(mine, wide[8 * q : 8 * q + 8, :], 0.0), axis=0, keepdims=True)
            rank = flat[:, 0:256]
            there = flat[:, 256:512]
            weight = flat[:, 512:768]
            group = (lax.broadcasted_iota(jnp.int32, (1, 256), 1) >> 5) * 8
            key = jnp.where(there > 0.5, group.astype(F32) + rank, -1.0)
            slot = lax.broadcasted_iota(jnp.int32, (64, 256), 0).astype(F32)
            pick = slot == key
            scale = jnp.sum(jnp.where(pick, weight, 0.0), axis=1, keepdims=True)
            one = jnp.where(pick, 1.0, 0.0).astype(BF16)
            sel[2 * g + q] = one
            base = 8 * g + 4 * q
            low = buf[pl.ds(base, 4), :, pl.ds(0, 32), :].reshape(256, 128)
            high = buf[pl.ds(base, 4), :, pl.ds(32, 32), :].reshape(256, 128)
            rows = pl.ds(16 * base, 64)
            sg[rows, 0:128] = (jnp.dot(one, low, preferred_element_type=F32) * scale).astype(BF16)
            sg[rows, 128:256] = (jnp.dot(one, high, preferred_element_type=F32) * scale).astype(BF16)
        grads = sg[pl.ds(128 * g, 128), :]
        for h in range(2):
            sums = lax.dot_general(grads, wd[pl.ds(512 * h, 512), :], LAST, preferred_element_type=F32)
            part[g, :, h] = sums.astype(BF16).reshape(8, 16, 512)

    def rs(g, j):
        dev = peer(j)
        p = dev[0]
        return remote(part.at[g, p // 2, p % 2], rsr.at[g, j], rss.at[g], rsrs.at[g], dev)

    def ag(g, j):
        piece = hg.at[g, d // 2, d % 2]
        return remote(piece, piece, ags.at[g], agr.at[g], peer(j))

    def rs_start(g):
        @pl.loop(1, n_dp)
        def _(j):
            rs(g, j).start()

    def rs_all(g):
        block = rsr.at[g, pl.ds(1, n_dp - 1)]
        return remote(block, block, rss.at[g], rsrs.at[g], sibling)

    def ag_all(g):
        block = rsr.at[g, pl.ds(1, n_dp - 1)]
        return remote(block, block, ags.at[g], agr.at[g], sibling)

    def reduce(g):
        rs_all(g).wait_recv()
        total = part[g, d // 2, d % 2].astype(F32)
        for j in range(1, n_dp):
            total = total + rsr[g, j].astype(F32)
        hg[g, d // 2, d % 2] = total.astype(BF16)

        @pl.loop(1, n_dp)
        def _(j):
            ag(g, j).start()

    def local(g):
        ag_all(g).wait_recv()
        rows = pl.ds(128 * g, 128)
        for h in range(2):
            cols = pl.ds(512 * h, 512)
            grad = hg[g, :, h].reshape(128, 512).astype(F32)
            dg[rows, cols] = (grad * fac_a[rows, cols]).astype(BF16)
            du[rows, cols] = (grad * fac_b[rows, cols]).astype(BF16)
        out = lax.dot_general(dg[rows, :], wg[...], LAST, preferred_element_type=F32)
        out = out + lax.dot_general(du[rows, :], wu[...], LAST, preferred_element_type=F32)
        out = out.astype(BF16)
        for q in range(2):
            dense = lax.dot_general(
                sel[2 * g + q], out[64 * q : 64 * q + 64, :], FIRST, preferred_element_type=F32
            )
            contr[pl.ds(8 * g + 4 * q, 4)] = dense.astype(BF16).reshape(4, 2, 32, 256)
        pair(g).start()

    def pair(g):
        block = pl.ds(8 * g, 8)
        return remote(contr.at[block, 1 - c], sb.at[block], cs.at[g], cr.at[g], sibling)

    def back(o):
        k = PARENT[o]
        i = PLACE[o]
        return remote(ssum.at[i], rb.at[i], zs2.at[0], zr2.at[i], chip(o - k))

    def join(g):
        pair(g).wait_recv()
        block = pl.ds(8 * g, 8)
        ssum[block] = (contr[block, c].astype(F32) + sb[block].astype(F32)).astype(BF16)
        for o in CHUNKS[g]:
            if o not in TREE:
                back(o).start()

    def forward(*ks):
        for k in ks:
            ssum[PLACE[k]] = gather(k).astype(BF16)
            back(k).start()

    def gather(k):
        total = ssum[PLACE[k]].astype(F32)
        for o in TREE[k][::-1]:
            back(o).wait_recv()
            total = total + rb[PLACE[o]].astype(F32)
        return total

    def pass_on(*ks):
        for k in ks:
            hop(k).wait_recv()
            relay(k)

    def leaves(g):
        for o in CHUNKS[g]:
            if o not in TREE:
                hop(o).wait_recv()
        share(g).start()

    pass_on(2, -2, 6, -6)
    leaves(0)
    share(0).wait_recv()
    scatter(0)
    rs_start(0)
    pass_on(8, -8, 5, -5)
    leaves(1)
    pass_on(12, -12)
    share(1).wait_recv()
    scatter(1)
    rs_start(1)
    pass_on(14, -14, 11, -11)
    leaves(2)
    reduce(0)
    share(2).wait_recv()
    scatter(2)
    rs_start(2)
    leaves(3)
    share(3).wait_recv()
    scatter(3)
    rs_start(3)
    load_wg.wait()
    load_wu.wait()
    local(0)
    reduce(2)
    join(0)
    reduce(3)
    reduce(1)
    local(2)
    join(2)
    local(3)
    forward(2, -2)
    join(3)
    local(1)
    forward(14, -14, 11, -11)
    join(1)
    forward(12, -12)
    forward(5, -5, 8, -8)

    load_xin.wait()
    for i, o in enumerate(ORDER):
        xin[pl.ds(16 * i, 16), :] = xin_by_chip[rows_of(o), :]

    @pl.loop(0, 4)
    def _(i):
        cols = pl.ds(pl.multiple_of(i * 256, 256), 256)
        gg[:, cols] = lax.dot_general(
            xin[...], dg[:, cols], FIRST, preferred_element_type=F32
        ).astype(BF16)
        gu[:, cols] = lax.dot_general(
            xin[...], du[:, cols], FIRST, preferred_element_type=F32
        ).astype(BF16)
        gd[cols, :] = lax.dot_general(
            hid[:, cols], sg[...], FIRST, preferred_element_type=F32
        ).astype(BF16)

    outs = [
        pltpu.make_async_copy(gg, gg_out, osem.at[0]),
        pltpu.make_async_copy(gu, gu_out, osem.at[1]),
        pltpu.make_async_copy(gd, gd_out, osem.at[2]),
    ]
    for cp in outs:
        cp.start()
    hops = buf.at[pl.ds(1, n_z - 1), c]
    remote(hops, hops, zs.at[0], zr.at[0], sibling).wait_send()
    for g in range(NCH):
        share(g).wait_send()
        pair(g).wait_send()
        rs_all(g).wait_send()
        ag_all(g).wait_send()
    forward(6, -6)
    gin[...] = gather(0).astype(BF16)
    last = pltpu.make_async_copy(gin, gin_out, osem.at[3])
    last.start()

    hops = rb.at[pl.ds(1, n_z - 1)]
    remote(hops, hops, zs2.at[0], zr2.at[0], sibling).wait_send()
    for cp in outs:
        cp.wait()
    last.wait()


def hand_over(*refs):
    sources, targets, held, sem = refs[:4], refs[4:8], refs[8:12], refs[12]
    loads, stores = [], []
    for i in range(4):
        parts = 2 if i else 1
        rows = sources[i].shape[0] // parts
        for part in range(parts):
            block = pl.ds(rows * part, rows)
            here = held[i].at[block]
            loads.append(pltpu.make_async_copy(sources[i].at[block], here, sem.at[0, i, part]))
            stores.append(pltpu.make_async_copy(here, targets[i].at[block], sem.at[1, i, part]))
    for load in loads:
        load.start()
    for load, store in zip(loads, stores):
        load.wait()
        store.start()
    for store in stores:
        store.wait()


def solution(mesh):
    n_dp = mesh.shape["dp"]
    n_z = mesh.shape["expert"] // 2

    def on_device(grad_out, routes, route_weight, saved_input, saved_gate, saved_up, w_gate, w_up, w_down):
        anywhere = pl.BlockSpec(memory_space=pl.ANY)
        dma = pltpu.SemaphoreType.DMA
        vm = pltpu.VMEM
        grads = pl.pallas_call(
            lambda *refs: kernel(n_dp, n_z, *refs),
            out_shape=(
                jax.ShapeDtypeStruct((32, 256), BF16),
                jax.ShapeDtypeStruct((256, 1024), BF16),
                jax.ShapeDtypeStruct((256, 1024), BF16),
                jax.ShapeDtypeStruct((1024, 256), BF16),
            ),
            in_specs=[anywhere] + [pl.BlockSpec(memory_space=pltpu.VMEM)] * 2 + [anywhere] * 6,
            out_specs=[anywhere] * 4,
            scratch_shapes=[
                vm((32, 2, 80, 128), BF16),
                vm((512, 256), BF16),
                vm((512, 256), BF16),
                vm((512, 1024), BF16),
                vm((512, 1024), BF16),
                vm((256, 1024), BF16),
                vm((256, 1024), BF16),
                vm((1024, 256), BF16),
                vm((512, 1024), F32),
                vm((512, 1024), F32),
                vm((512, 1024), BF16),
                vm((8, 64, 256), BF16),
                vm((512, 256), BF16),
                vm((NCH, 8, 2, 16, 512), BF16),
                vm((NCH, 16, 16, 512), BF16),
                vm((NCH, 8, 2, 16, 512), BF16),
                vm((512, 1024), BF16),
                vm((512, 1024), BF16),
                vm((32, 2, 32, 256), BF16),
                vm((32, 32, 256), BF16),
                vm((32, 32, 256), BF16),
                vm((32, 32, 256), BF16),
                vm((32, 256), BF16),
                vm((256, 1024), BF16),
                vm((256, 1024), BF16),
                vm((1024, 256), BF16),
                dma((9,)),
                dma((4,)),
                dma((1,)),
                dma((32,)),
                dma((NCH,)),
                dma((NCH,)),
                dma((NCH,)),
                dma((NCH,)),
                dma((NCH,)),
                dma((NCH,)),
                dma((NCH,)),
                dma((NCH,)),
                dma((1,)),
                dma((32,)),
            ],
            name="expert_backward",
            compiler_params=pltpu.CompilerParams(
                collective_id=0, has_side_effects=True, vmem_limit_bytes=56 * 1024 * 1024
            ),
        )(
            grad_out,
            routes.T,
            route_weight.T,
            saved_input[0],
            saved_gate[0],
            saved_up[0],
            w_gate[0],
            w_up[0],
            w_down[0],
        )
        grad_in, grad_gate, grad_up, grad_down = pl.pallas_call(
            hand_over,
            out_shape=tuple(jax.ShapeDtypeStruct(a.shape, a.dtype) for a in grads),
            in_specs=[anywhere] * 4,
            out_specs=[anywhere] * 4,
            scratch_shapes=[vm(a.shape, a.dtype) for a in grads] + [dma((2, 4, 2))],
            name="hand_over",
            compiler_params=pltpu.CompilerParams(vmem_limit_bytes=56 * 1024 * 1024),
        )(*grads)
        return (grad_in, grad_gate[None], grad_up[None], grad_down[None])

    in_specs = (
        P("expert", "dp"),
        P("expert", None),
        P("expert", None),
        P("expert", None, "dp"),
        P("expert", None, None),
        P("expert", None, None),
        P("expert", "dp", None),
        P("expert", "dp", None),
        P("expert", None, "dp"),
    )
    out_specs = (
        P("expert", "dp"),
        P("expert", "dp", None),
        P("expert", "dp", None),
        P("expert", None, "dp"),
    )
    return jax.shard_map(
        on_device, mesh=mesh, in_specs=in_specs, out_specs=out_specs, check_vma=False
    )
```
